256 devices in a mesh: row: 8 (over y_lo, x), col: 4 (over y_hi, core), dep: 8 (over z).
Axes of the slice: x: 4, y: 4 (y_hi: 2, y_lo: 2; y = y_hi * 2 + y_lo), z: 8, core: 2. Of those that a mesh axis runs over, the one named last changes fastest.
Arguments:
- tokens_in: bfloat16 [8, 384, 6144], P('dep', None, 'row'), may hold values from -6 to 6
- weight: bfloat16 [6144, 24576], P('row', 'col'), may hold values from -0.078125 to 0.078125
- cotangent: bfloat16 [8, 384, 24576], P('dep', 'row', 'col'), may hold values from -6 to 6
Outputs:
- activated: bfloat16 [8, 384, 24576], P('dep', 'row', 'col')
- input_grad: bfloat16 [8, 384, 6144], P('dep', 'col', 'row')
- weight_grad: bfloat16 [6144, 24576], P(('row', 'dep'), 'col')
The draws below stay inside these ranges and needn't reach their ends.
All inputs are finite; a program needn't handle non-finite values.
Results may differ from the reference program's by a relative error of at most 0.023.
Values may be sent and summed in bfloat16 or wider, within the bound.
A program may use at most 128 MiB of HBM per device.

```python
import math
import jax
import jax.numpy as jnp
from jax import lax

D = 6144
FF = 24576
DEP_TOK = 384
N_DEP = 8


def levels(own_key, dims, split, low, largest):
    gain = 1.0
    for position, parts in split:
        steps = jax.random.uniform(jax.random.fold_in(jax.random.fold_in(own_key, 6), position), (parts,), jnp.float32, low / len(split), largest / len(split))
        gain = gain * jnp.repeat(jnp.exp(steps), dims[position] // parts).reshape((-1,) + (1,) * (len(dims) - 1 - position))
    return gain


def gaussian(rng, dims, width, limit, shards=(), kind=jnp.bfloat16):
    result = width * jax.random.normal(rng, dims, jnp.float32)
    if shards:
        result = result * levels(rng, dims, shards, -0.22, 0.18)
    return jnp.clip(result, -limit, limit).astype(kind)


def setup_inputs(seed: int = 0) -> dict:
    key_list = jax.random.split(jax.random.key(seed), 4)
    return {
        "tokens_in": gaussian(key_list[0], (N_DEP, DEP_TOK, D), 1.0, 6.0, ((0, 8), (2, 8))),
        "weight": gaussian(key_list[1], (D, FF), D ** -0.5, 0.078125, ((0, 8), (1, 4))),
        "cotangent": gaussian(key_list[2], (N_DEP, DEP_TOK, FF), 1.0, 6.0, ((0, 8), (1, 8), (2, 4))),
    }


root_coef = math.sqrt(2.0 / math.pi)

def slope_of(value):
    inner = root_coef * (value + 0.044715 * value * value * value)
    tangent = jnp.tanh(inner)
    return 0.5 * (1.0 + tangent) + 0.5 * value * (1.0 - tangent * tangent) * root_coef * (1.0 + 3.0 * 0.044715 * value * value)

def reference(tokens_in, weight, cotangent):
    scale = 1.0 / math.sqrt(tokens_in.shape[0] * tokens_in.shape[1])

    def one_group(carry, pair):
        group_tokens, group_cot = pair
        pre_act = jnp.dot(group_tokens, weight, preferred_element_type=jnp.float32)
        activated = jax.nn.gelu(pre_act, approximate=True).astype(jnp.bfloat16)
        hidden_grad = (group_cot.astype(jnp.float32) * slope_of(pre_act)).astype(jnp.bfloat16)
        grad_in = lax.dot_general(hidden_grad, weight, (((1,), (1,)), ((), ())), preferred_element_type=jnp.float32).astype(jnp.bfloat16)
        group_grad = (lax.dot_general(group_tokens, hidden_grad, (((0,), (0,)), ((), ())), preferred_element_type=jnp.float32) * scale).astype(jnp.bfloat16)
        group_grad = lax.optimization_barrier(group_grad)
        return (carry + group_grad.astype(jnp.float32), (activated, grad_in))
    total, (activated, input_grad) = lax.scan(one_group, jnp.zeros(weight.shape, jnp.float32), (tokens_in, cotangent))
    return (activated, input_grad, total.astype(jnp.bfloat16))
```

```python
import functools
import math

import jax
import jax.numpy as jnp
from jax import lax
from jax.experimental import pallas as pl
from jax.experimental.pallas import tpu as pltpu
from jax.sharding import PartitionSpec as P

MESH = pl.DeviceIdType.MESH
F32 = jnp.float32
BF16 = jnp.bfloat16

CHUNKS = 8

root_coef = math.sqrt(2.0 / math.pi)

RS1, RS2, RSY, AGY, AGX1, AGX2, Z1, Z2, Z3, Z4 = 0, 2, 4, 5, 6, 8, 10, 12, 14, 16
COPIES = 18


def kernel(
    scale, chunks,
    tok_hbm, w_hbm, cot_hbm, act_hbm, ig_hbm, wg_hbm,
    tok, tok_t, w, cot, part, r1, r2, y_out, y_in, own, hid, grad, z1_in, z_in,
    acc, ig_out, ig_in, ig_own, act, wg,
    send, recv, col_send, col_recv, load_w, load_cot, load_tok, store_act, store_wg, store_ig,
):
    width = w.shape[2]
    half = width // 2
    left_half, right_half = pl.ds(0, half), pl.ds(half, half)
    row, col, dep = lax.axis_index("row"), lax.axis_index("col"), lax.axis_index("dep")
    x, y = lax.rem(row, 4), row // 4
    other_y = 1 - y
    xr, xo, xl = lax.rem(x + 1, 4), lax.rem(x + 2, 4), lax.rem(x + 3, 4)
    right, left = {"row": y * 4 + xr}, {"row": y * 4 + xl}
    across = {"row": other_y * 4 + x}
    at = [lax.rem(dep + k, 8) for k in range(8)]
    up, down = {"dep": at[1]}, {"dep": at[7]}
    col_peers = [{"col": lax.rem(col + j, 4)} for j in (1, 2, 3)]

    def columns(c):
        return pl.ds(pl.multiple_of(c * width, 128), width)

    def tok_copy():
        return pltpu.make_async_copy(tok_hbm.at[0], tok, load_tok)

    def w_copy(c):
        return pltpu.make_async_copy(w_hbm.at[:, columns(c)], w.at[c], load_w.at[c])

    def cot_copy(c):
        return pltpu.make_async_copy(cot_hbm.at[0, :, columns(c)], cot.at[c], load_cot.at[c])

    tok_copy().start()

    @pl.loop(0, chunks)
    def _(c):
        w_copy(c).start()

    @pl.loop(0, chunks)
    def _(c):
        cot_copy(c).start()

    barrier = pltpu.get_barrier_semaphore()
    peers = [right, left, across, up, down] + col_peers
    for peer in peers:
        pl.semaphore_signal(barrier, inc=1, device_id=peer, device_id_type=MESH)

    def act_copy(c):
        return pltpu.make_async_copy(act.at[c], act_hbm.at[0, :, columns(c)], store_act.at[c])

    def wg_copy(c):
        return pltpu.make_async_copy(wg.at[c], wg_hbm.at[:, columns(c)], store_wg.at[c])

    def ig_copy():
        return pltpu.make_async_copy(ig_own, ig_hbm.at[0], store_ig)

    def remote(c, which, source, target, device):
        return pltpu.make_async_remote_copy(
            src_ref=source, dst_ref=target, send_sem=send.at[c, which], recv_sem=recv.at[c, which],
            device_id=device, device_id_type=MESH,
        )

    def rs1(c):
        return (
            remote(c, RS1, part.at[c, :, xo, :, left_half], r1.at[c, 0], right),
            remote(c, RS1 + 1, part.at[c, :, xo, :, right_half], r1.at[c, 1], left),
        )

    def rs2(c):
        return (
            remote(c, RS2, part.at[c, :, xr], r2.at[c, 0], right),
            remote(c, RS2 + 1, part.at[c, :, xl], r2.at[c, 1], left),
        )

    def rsy(c):
        return (remote(c, RSY, y_out.at[c], y_in.at[c], across),)

    def agy(c):
        return (remote(c, AGY, hid.at[c, y, x], hid.at[c, y, x], across),)

    def agx1(c):
        return (
            remote(c, AGX1, hid.at[c, :, x], hid.at[c, :, x], right),
            remote(c, AGX1 + 1, hid.at[c, :, x], hid.at[c, :, x], left),
        )

    def agx2(c):
        return (
            remote(c, AGX2, hid.at[c, :, xl, :, left_half], hid.at[c, :, xl, :, left_half], right),
            remote(c, AGX2 + 1, hid.at[c, :, xr, :, right_half], hid.at[c, :, xr, :, right_half], left),
        )

    def z1(c):
        return (
            remote(c, Z1, grad.at[c, at[4], :, left_half], z1_in.at[c, 0], up),
            remote(c, Z1 + 1, grad.at[c, at[4], :, right_half], z1_in.at[c, 1], down),
        )

    def z_step(c, which, step, above, below):
        return (
            remote(c, which, grad.at[c, above], z_in.at[c, step, 0], up),
            remote(c, which + 1, grad.at[c, below], z_in.at[c, step, 1], down),
        )

    def z2(c):
        return z_step(c, Z2, 0, at[3], at[5])

    def z3(c):
        return z_step(c, Z3, 1, at[2], at[6])

    def z4(c):
        return z_step(c, Z4, 2, at[1], at[7])

    def start(copies):
        for copy in copies:
            copy.start()

    def arrived(copies):
        for copy in copies:
            copy.wait_recv()

    def col_copy(j):
        return pltpu.make_async_remote_copy(
            src_ref=ig_out.at[lax.rem(col + j, 4)], dst_ref=ig_in.at[j - 1],
            send_sem=col_send.at[j - 1], recv_sem=col_recv.at[j - 1],
            device_id=col_peers[j - 1], device_id_type=MESH,
        )

    def f32(value):
        return value.astype(F32)

    def project(c):
        w_copy(c).wait()
        block = jnp.dot(tok[...], w[c], preferred_element_type=F32).astype(BF16)
        part[c] = block.reshape(part.shape[1:])
        start(rs1(c))

    def row_second(c):
        arrived(rs1(c))
        part[c, :, xr, :, left_half] = (f32(part[c, :, xr, :, left_half]) + f32(r1[c, 0])).astype(BF16)
        part[c, :, xl, :, right_half] = (f32(part[c, :, xl, :, right_half]) + f32(r1[c, 1])).astype(BF16)
        start(rs2(c))

    def row_across(c):
        arrived(rs2(c))
        y_out[c] = (f32(part[c, other_y, x]) + f32(r2[c, 0, other_y]) + f32(r2[c, 1, other_y])).astype(BF16)
        start(rsy(c))
        own[c] = f32(part[c, y, x]) + f32(r2[c, 0, y]) + f32(r2[c, 1, y])

    def activate(c):
        arrived(rsy(c))
        cot_copy(c).wait()
        value = own[c] + f32(y_in[c])
        square = value * value
        tangent = jnp.tanh(root_coef * (value + 0.044715 * value * square))
        slope = 0.5 * (1.0 + tangent) + 0.5 * value * (1.0 - tangent * tangent) * root_coef * (
            1.0 + 3.0 * 0.044715 * square
        )
        hid[c, y, x] = (f32(cot[c]) * slope).astype(BF16)
        start(agy(c))
        act[c] = (0.5 * value * (1.0 + tangent)).astype(BF16)
        act_copy(c).start()

    def gather_first(c):
        arrived((remote(c, AGY, hid.at[c, other_y, x], hid.at[c, other_y, x], across),))
        start(agx1(c))

    def gather_second(c):
        arrived((
            remote(c, AGX1, hid.at[c, :, xl], hid.at[c, :, xl], right),
            remote(c, AGX1 + 1, hid.at[c, :, xr], hid.at[c, :, xr], left),
        ))
        start(agx2(c))

    def weight_first(c):
        arrived((
            remote(c, AGX2, hid.at[c, :, xo, :, left_half], hid.at[c, :, xo, :, left_half], right),
            remote(c, AGX2 + 1, hid.at[c, :, xo, :, right_half], hid.at[c, :, xo, :, right_half], left),
        ))
        rows = hid[c].reshape(-1, width)
        product = jnp.dot(tok_t[...], rows, preferred_element_type=F32)
        grad[c] = (product * scale).astype(BF16).reshape(grad.shape[1:])
        start(z1(c))

    def input_part(c):
        rows = hid[c].reshape(-1, width)
        acc[...] += lax.dot_general(rows, w[c], (((1,), (1,)), ((), ())), preferred_element_type=F32)

        @pl.when(c == chunks - 1)
        def _():
            ig_out[...] = acc[...].astype(BF16).reshape(ig_out.shape)
            for j in (1, 2, 3):
                col_copy(j).start()

    def weight_second(c):
        arrived(z1(c))
        grad[c, at[3], :, left_half] = (f32(grad[c, at[3], :, left_half]) + f32(z1_in[c, 0])).astype(BF16)
        grad[c, at[5], :, right_half] = (f32(grad[c, at[5], :, right_half]) + f32(z1_in[c, 1])).astype(BF16)
        start(z2(c))

    def weight_third(c):
        arrived(z2(c))
        grad[c, at[2]] = (f32(grad[c, at[2]]) + f32(z_in[c, 0, 0])).astype(BF16)
        grad[c, at[6]] = (f32(grad[c, at[6]]) + f32(z_in[c, 0, 1])).astype(BF16)
        start(z3(c))

    def weight_fourth(c):
        arrived(z3(c))
        grad[c, at[1]] = (f32(grad[c, at[1]]) + f32(z_in[c, 1, 0])).astype(BF16)
        grad[c, at[7]] = (f32(grad[c, at[7]]) + f32(z_in[c, 1, 1])).astype(BF16)
        start(z4(c))

    def weight_last(c):
        arrived(z4(c))
        wg[c] = (f32(grad[c, dep]) + f32(z_in[c, 2, 0]) + f32(z_in[c, 2, 1])).astype(BF16)
        wg_copy(c).start()

    tok_copy().wait()
    tok_t[...] = tok[...].T
    acc[...] = jnp.zeros_like(acc)
    pl.semaphore_wait(barrier, len(peers))

    order = (
        (weight_first, 2), (activate, 1), (project, 0), (input_part, 2),
        (weight_third, 3), (gather_first, 1),
        (weight_second, 2), (row_second, 0),
        (weight_fourth, 3), (gather_second, 1), (row_across, 0), (weight_last, 4),
    )
    slots = max(late for _, late in order)

    @pl.loop(0, chunks + slots)
    def _(t):
        for stage, late in order:
            c = t - late

            @pl.when((c >= 0) & (c < chunks))
            def _(stage=stage, c=c):
                stage(c)

    for j in (1, 2, 3):
        col_copy(j).wait_recv()
    tokens = ig_own.shape[0]
    mine = acc[pl.ds(pl.multiple_of(col * tokens, 8), tokens), :]
    ig_own[...] = (mine + f32(ig_in[0]) + f32(ig_in[1]) + f32(ig_in[2])).astype(BF16)
    ig_copy().start()

    @pl.loop(0, chunks)
    def _(c):
        for copies in (rs1, rs2, rsy, agy, agx1, agx2, z1, z2, z3, z4):
            for copy in copies(c):
                copy.wait_send()
        act_copy(c).wait()
        wg_copy(c).wait()

    for j in (1, 2, 3):
        col_copy(j).wait_send()
    ig_copy().wait()


def body(chunks, tokens_in, weight, cotangent):
    tokens, features = tokens_in.shape[1:]
    hidden = weight.shape[1]
    own_tokens = cotangent.shape[1]
    scale = 1.0 / math.sqrt(tokens * lax.axis_size("dep"))
    c, w = chunks, hidden // chunks
    h = w // 2
    own_features, col_tokens = features // 8, tokens // 4
    vmem = pltpu.VMEM
    dma = pltpu.SemaphoreType.DMA
    return pl.pallas_call(
        functools.partial(kernel, scale, chunks),
        out_shape=(
            jax.ShapeDtypeStruct((1, own_tokens, hidden), BF16),
            jax.ShapeDtypeStruct((1, col_tokens, features), BF16),
            jax.ShapeDtypeStruct((own_features, hidden), BF16),
        ),
        in_specs=[pl.BlockSpec(memory_space=pl.ANY)] * 3,
        out_specs=(pl.BlockSpec(memory_space=pl.ANY),) * 3,
        scratch_shapes=[
            vmem((tokens, features), BF16),
            vmem((features, tokens), BF16),
            vmem((c, features, w), BF16),
            vmem((c, own_tokens, w), BF16),
            vmem((c, 2, 4, own_tokens, w), BF16),
            vmem((c, 2, 2, own_tokens, h), BF16),
            vmem((c, 2, 2, own_tokens, w), BF16),
            vmem((c, own_tokens, w), BF16),
            vmem((c, own_tokens, w), BF16),
            vmem((c, own_tokens, w), F32),
            vmem((c, 2, 4, own_tokens, w), BF16),
            vmem((c, 8, own_features, w), BF16),
            vmem((c, 2, own_features, h), BF16),
            vmem((c, 3, 2, own_features, w), BF16),
            vmem((tokens, features), F32),
            vmem((4, col_tokens, features), BF16),
            vmem((3, col_tokens, features), BF16),
            vmem((col_tokens, features), BF16),
            vmem((c, own_tokens, w), BF16),
            vmem((c, own_features, w), BF16),
            dma((c, COPIES)),
            dma((c, COPIES)),
            dma((3,)),
            dma((3,)),
            dma((c,)),
            dma((c,)),
            dma,
            dma((c,)),
            dma((c,)),
            dma,
        ],
        compiler_params=pltpu.CompilerParams(
            collective_id=0, has_side_effects=True, vmem_limit_bytes=60 * 1024 * 1024
        ),
        cost_estimate=pl.CostEstimate(
            flops=6 * tokens * features * hidden,
            bytes_accessed=2 * (features * hidden + 2 * own_tokens * hidden + tokens * features),
            transcendentals=own_tokens * hidden,
        ),
    )(tokens_in, weight, cotangent)


def solution(mesh):
    in_specs = (P("dep", None, "row"), P("row", "col"), P("dep", "row", "col"))
    out_specs = (P("dep", "row", "col"), P("dep", "col", "row"), P(("row", "dep"), "col"))
    return jax.shard_map(
        functools.partial(body, CHUNKS), mesh=mesh, in_specs=in_specs, out_specs=out_specs, check_vma=False
    )
```

```python
import functools
import math

import jax
import jax.numpy as jnp
from jax import lax
from jax.experimental import pallas as pl
from jax.experimental.pallas import tpu as pltpu
from jax.sharding import PartitionSpec as P

MESH = pl.DeviceIdType.MESH
F32 = jnp.float32
BF16 = jnp.bfloat16

WIDTH = 512

root_coef = math.sqrt(2.0 / math.pi)

RS1, RS2, RSY, AG1, AG2, AG3, Z1, Z2, Z3, Z4 = 0, 2, 4, 5, 8, 12, 13, 15, 17, 19
COPIES = 21

PLAN = (
    1, 2, 33, 384, 34, 65, 3, 97, 66, 35, 192, 129, 98, 4, 161, 67, 256, 130, 36, 193, 99, 5, 162, 288,
    68, 224, 257, 131, 37, 194, 100, 320, 6, 163, 289, 69, 225, 258, 132, 38, 195, 352, 101, 321, 7,
    164, 290, 70, 226, 259, 133, 39, 196, 353, 102, 322, 8, 165, 291, 71, 227, 260, 134, 40, 197, 354,
    103, 323, 9, 166, 292, 72, 228, 261, 135, 41, 198, 355, 104, 324, 10, 167, 293, 73, 229, 262, 136,
    42, 199, 356, 105, 325, 11, 168, 294, 74, 230, 263, 137, 43, 200, 357, 106, 326, 169, 295, 75, 231,
    264, 138, 201, 358, 107, 327, 170, 296, 232, 265, 139, 202, 359, 328, 171, 297, 233, 266, 203, 360,
    329, 298, 234, 267, 361, 330, 299, 235, 362, 331, 363,
)
STAGE_OF_INPUT_PART = 7
LAST_INPUT_PART = [entry % 32 for entry in PLAN if entry // 32 == STAGE_OF_INPUT_PART][-1]


def kernel(
    scale, chunks,
    tok_hbm, w_hbm, cot_hbm, act_hbm, ig_hbm, wg_hbm,
    tok, tok_t, w, cot, part, r1, r2, y_out, y_in, own, hid, grad, z1_in, z_in, direct_in,
    acc, ig_out, ig_in, ig_own, act, wg,
    send, recv, direct_send, direct_recv, col_send, col_recv, load_w, load_cot, load_tok,
    store_act, store_wg, store_ig,
):
    width = w.shape[2]
    half = width // 2
    left_half, right_half = pl.ds(0, half), pl.ds(half, half)
    row, col, dep = lax.axis_index("row"), lax.axis_index("col"), lax.axis_index("dep")
    x, y = lax.rem(row, 4), row // 4
    other_y = 1 - y
    xr, xo, xl = lax.rem(x + 1, 4), lax.rem(x + 2, 4), lax.rem(x + 3, 4)
    right, left = {"row": y * 4 + xr}, {"row": y * 4 + xl}
    across = {"row": other_y * 4 + x}
    at = [lax.rem(dep + k, 8) for k in range(8)]
    up, down = {"dep": at[1]}, {"dep": at[7]}
    row_peers = [(lax.rem(y + k // 4, 2), lax.rem(x + k % 4, 4)) for k in (6, 2, 5, 7, 1, 3, 4)]
    row_from = [(lax.rem(y + k // 4, 2), lax.rem(x + 4 - k % 4, 4)) for k in (6, 2, 5, 7, 1, 3, 4)]
    col_peers = [{"col": lax.rem(col + j, 4)} for j in (1, 2, 3)]

    def columns(c):
        return pl.ds(pl.multiple_of(c * width, 128), width)

    def tok_copy():
        return pltpu.make_async_copy(tok_hbm.at[0], tok, load_tok)

    def w_copy(c):
        return pltpu.make_async_copy(w_hbm.at[:, columns(c)], w.at[c], load_w.at[c])

    def cot_copy(c):
        return pltpu.make_async_copy(cot_hbm.at[0, :, columns(c)], cot.at[c], load_cot.at[c])

    tok_copy().start()

    @pl.loop(0, chunks)
    def _(c):
        w_copy(c).start()
        cot_copy(c).start()

    barrier = pltpu.get_barrier_semaphore()
    peers = [up, down] + [{"row": there_y * 4 + there_x} for there_y, there_x in row_peers] + col_peers
    for peer in peers:
        pl.semaphore_signal(barrier, inc=1, device_id=peer, device_id_type=MESH)

    def act_copy(c):
        return pltpu.make_async_copy(act.at[c], act_hbm.at[0, :, columns(c)], store_act.at[c])

    def wg_copy(c):
        return pltpu.make_async_copy(wg.at[c], wg_hbm.at[:, columns(c)], store_wg.at[c])

    def ig_copy():
        return pltpu.make_async_copy(ig_own, ig_hbm.at[0], store_ig)

    def remote(c, which, source, target, device):
        return pltpu.make_async_remote_copy(
            src_ref=source, dst_ref=target, send_sem=send.at[c, which], recv_sem=recv.at[c, which],
            device_id=device, device_id_type=MESH,
        )

    def direct(k, source, target):
        there_y, there_x = row_peers[k % 7]
        return pltpu.make_async_remote_copy(
            src_ref=source, dst_ref=target, send_sem=direct_send.at[k], recv_sem=direct_recv.at[k],
            device_id={"row": there_y * 4 + there_x}, device_id_type=MESH,
        )

    def direct_scatter():
        return [direct(k, part.at[0, *row_peers[k]], direct_in.at[k]) for k in range(7)]

    def direct_gather():
        return [direct(7 + k, hid.at[0, y, x], hid.at[0, y, x]) for k in range(7)]

    def direct_gathered():
        return [direct(7 + k, hid.at[0, *row_from[k]], hid.at[0, *row_from[k]]) for k in range(7)]

    def rs1(c):
        return (
            remote(c, RS1, part.at[c, :, xo, :, left_half], r1.at[c, 0], right),
            remote(c, RS1 + 1, part.at[c, :, xo, :, right_half], r1.at[c, 1], left),
        )

    def rs2(c):
        return (
            remote(c, RS2, part.at[c, :, xr], r2.at[c, 0], right),
            remote(c, RS2 + 1, part.at[c, :, xl], r2.at[c, 1], left),
        )

    def rsy(c):
        return (remote(c, RSY, y_out.at[c], y_in.at[c], across),)

    def block(c, which, there, device, columns=None):
        ref = hid.at[c, *there] if columns is None else hid.at[c, *there, :, columns]
        return remote(c, which, ref, ref, device)

    def ag1(c, here=True):
        return (
            block(c, AG1, (y, x if here else xl), right),
            block(c, AG1 + 1, (y, x if here else xr), left),
            block(c, AG1 + 2, (y if here else other_y, x), across),
        )

    def ag2(c, here=True):
        return (
            block(c, AG2, (y, xl if here else xo), right, left_half),
            block(c, AG2 + 1, (y, xr if here else xo), left, right_half),
            block(c, AG2 + 2, (y if here else other_y, xl), across),
            block(c, AG2 + 3, (y if here else other_y, xr), across),
        )

    def ag3(c, here=True):
        return (block(c, AG3, (y if here else other_y, xo), across),)

    def z1(c):
        return (
            remote(c, Z1, grad.at[c, at[4], :, left_half], z1_in.at[c, 0], up),
            remote(c, Z1 + 1, grad.at[c, at[4], :, right_half], z1_in.at[c, 1], down),
        )

    def z_step(c, which, step, above, below):
        return (
            remote(c, which, grad.at[c, above], z_in.at[c, step, 0], up),
            remote(c, which + 1, grad.at[c, below], z_in.at[c, step, 1], down),
        )

    def z2(c):
        return z_step(c, Z2, 0, at[3], at[5])

    def z3(c):
        return z_step(c, Z3, 1, at[2], at[6])

    def z4(c):
        return z_step(c, Z4, 2, at[1], at[7])

    def start(copies):
        for copy in copies:
            copy.start()

    def arrived(copies):
        for copy in copies:
            copy.wait_recv()

    def col_copy(j):
        return pltpu.make_async_remote_copy(
            src_ref=ig_out.at[lax.rem(col + j, 4)], dst_ref=ig_in.at[j - 1],
            send_sem=col_send.at[j - 1], recv_sem=col_recv.at[j - 1],
            device_id=col_peers[j - 1], device_id_type=MESH,
        )

    def f32(value):
        return value.astype(F32)

    def product_of(c):
        w_copy(c).wait()
        value = jnp.dot(tok[...], w[c], preferred_element_type=F32).astype(BF16)
        part[c] = value.reshape(part.shape[1:])

    def finish(c, value):
        square = value * value
        tangent = jnp.tanh(root_coef * (value + 0.044715 * value * square))
        slope = 0.5 * (1.0 + tangent) + 0.5 * value * (1.0 - tangent * tangent) * root_coef * (
            1.0 + 3.0 * 0.044715 * square
        )
        cot_copy(c).wait()
        hid[c, y, x] = (f32(cot[c]) * slope).astype(BF16)
        start(direct_gather() if isinstance(c, int) else ag1(c))
        act[c] = (0.5 * value * (1.0 + tangent)).astype(BF16)
        act_copy(c).start()

    def project(c):
        product_of(c)
        start(rs1(c))

    def row_second(c):
        arrived(rs1(c))
        part[c, :, xr, :, left_half] = (f32(part[c, :, xr, :, left_half]) + f32(r1[c, 0])).astype(BF16)
        part[c, :, xl, :, right_half] = (f32(part[c, :, xl, :, right_half]) + f32(r1[c, 1])).astype(BF16)
        start(rs2(c))

    def row_across(c):
        arrived(rs2(c))
        y_out[c] = (f32(part[c, other_y, x]) + f32(r2[c, 0, other_y]) + f32(r2[c, 1, other_y])).astype(BF16)
        start(rsy(c))
        own[c] = f32(part[c, y, x]) + f32(r2[c, 0, y]) + f32(r2[c, 1, y])

    def activate(c):
        arrived(rsy(c))
        finish(c, own[c] + f32(y_in[c]))

    def gather_second(c):
        arrived(ag1(c, False)[:2])
        start(ag2(c))

    def gather_third(c):
        arrived(ag2(c, False)[:2])
        start(ag3(c))

    def weight_first(c):
        @pl.when(c > 0)
        def _():
            arrived(ag1(c, False)[2:] + ag2(c, False)[2:] + ag3(c, False))

        @pl.when(c == 0)
        def _():
            arrived(direct_gathered())

        rows = hid[c].reshape(-1, width)
        product = jnp.dot(tok_t[...], rows, preferred_element_type=F32)
        grad[c] = (product * scale).astype(BF16).reshape(grad.shape[1:])
        start(z1(c))

    def input_part(c):
        rows = hid[c].reshape(-1, width)
        acc[...] += lax.dot_general(rows, w[c], (((1,), (1,)), ((), ())), preferred_element_type=F32)

        @pl.when(c == LAST_INPUT_PART)
        def _():
            ig_out[...] = acc[...].astype(BF16).reshape(ig_out.shape)
            for j in (1, 2, 3):
                col_copy(j).start()

    def weight_second(c):
        arrived(z1(c))
        grad[c, at[3], :, left_half] = (f32(grad[c, at[3], :, left_half]) + f32(z1_in[c, 0])).astype(BF16)
        grad[c, at[5], :, right_half] = (f32(grad[c, at[5], :, right_half]) + f32(z1_in[c, 1])).astype(BF16)
        start(z2(c))

    def weight_third(c):
        arrived(z2(c))
        grad[c, at[2]] = (f32(grad[c, at[2]]) + f32(z_in[c, 0, 0])).astype(BF16)
        grad[c, at[6]] = (f32(grad[c, at[6]]) + f32(z_in[c, 0, 1])).astype(BF16)
        start(z3(c))

    def weight_fourth(c):
        arrived(z3(c))
        grad[c, at[1]] = (f32(grad[c, at[1]]) + f32(z_in[c, 1, 0])).astype(BF16)
        grad[c, at[7]] = (f32(grad[c, at[7]]) + f32(z_in[c, 1, 1])).astype(BF16)
        start(z4(c))

    def weight_last(c):
        arrived(z4(c))
        wg[c] = (f32(grad[c, dep]) + f32(z_in[c, 2, 0]) + f32(z_in[c, 2, 1])).astype(BF16)
        wg_copy(c).start()

        def sent(stages_of_chunk):
            for copies in stages_of_chunk:
                for copy in copies(c):
                    copy.wait_send()

        sent((z1, z2, z3, z4))

        @pl.when(c > 0)
        def _():
            sent((rs1, rs2, rsy, ag1, ag2, ag3))

        @pl.when(c == 0)
        def _():
            for copy in direct_scatter() + direct_gather():
                copy.wait_send()

        act_copy(c).wait()

    def first_activate(_):
        arrived(direct_scatter())
        value = f32(part[0, y, x])
        for k in range(7):
            value = value + f32(direct_in[k])
        finish(0, value)

    tok_copy().wait()
    product_of(0)
    pl.semaphore_wait(barrier, len(peers))
    start(direct_scatter())
    tok_t[...] = tok[...].T
    acc[...] = jnp.zeros_like(acc)

    stages = (
        project, row_second, row_across, activate, gather_second, gather_third, weight_first,
        input_part, weight_second, weight_third, weight_fourth, weight_last, first_activate,
    )

    words = [
        sum(entry * 512 ** k for k, entry in enumerate(PLAN[i:i + 3])) for i in range(0, len(PLAN), 3)
    ]

    @pl.loop(0, len(PLAN))
    def _(i):
        place, level = i // 3, words
        while len(level) > 1:
            odd = lax.rem(place, 2) == 1
            pairs = [level[k:k + 2] for k in range(0, len(level), 2)]
            level = [jnp.where(odd, pair[-1], pair[0]) for pair in pairs]
            place = place // 2
        within = lax.rem(i, 3)
        word = jnp.where(within == 0, level[0], jnp.where(within == 1, level[0] // 512, level[0] // 262144))
        entry = lax.rem(word, 512)
        stage, c = entry // 32, lax.rem(entry, 32)

        def dispatch(low, high):
            if high - low == 1:
                stages[low](c)
                return
            middle = (low + high) // 2
            lax.cond(stage < middle, lambda: dispatch(low, middle), lambda: dispatch(middle, high))

        dispatch(0, len(stages))

    for j in (1, 2, 3):
        col_copy(j).wait_recv()
    tokens = ig_own.shape[0]
    mine = acc[pl.ds(pl.multiple_of(col * tokens, 8), tokens), :]
    ig_own[...] = (mine + f32(ig_in[0]) + f32(ig_in[1]) + f32(ig_in[2])).astype(BF16)
    ig_copy().start()

    @pl.loop(0, chunks)
    def _(c):
        wg_copy(c).wait()

    for j in (1, 2, 3):
        col_copy(j).wait_send()
    ig_copy().wait()


def publish(act_from, ig_from, wg_from, act_to, ig_to, wg_to, act, ig, wg, sem_in, sem_out):
    inward, outward = [], []
    for k, (source, held, target) in enumerate(((wg_from, wg, wg_to), (act_from, act, act_to), (ig_from, ig, ig_to))):
        inward.append(pltpu.make_async_copy(source, held, sem_in.at[k]))
        outward.append(pltpu.make_async_copy(held, target, sem_out.at[k]))
    for copy in inward:
        copy.start()
    for copy, onward in zip(inward, outward):
        copy.wait()
        onward.start()
    for copy in outward:
        copy.wait()


def body(tokens_in, weight, cotangent):
    tokens, features = tokens_in.shape[1:]
    hidden = weight.shape[1]
    own_tokens = cotangent.shape[1]
    scale = 1.0 / math.sqrt(tokens * lax.axis_size("dep"))
    c, w = hidden // WIDTH, WIDTH
    h = w // 2
    own_features, col_tokens = features // 8, tokens // 4
    vmem = pltpu.VMEM
    dma = pltpu.SemaphoreType.DMA
    results = pl.pallas_call(
        functools.partial(kernel, scale, c),
        out_shape=(
            jax.ShapeDtypeStruct((1, own_tokens, hidden), BF16),
            jax.ShapeDtypeStruct((1, col_tokens, features), BF16),
            jax.ShapeDtypeStruct((own_features, hidden), BF16),
        ),
        in_specs=[pl.BlockSpec(memory_space=pl.ANY)] * 3,
        out_specs=(pl.BlockSpec(memory_space=pl.ANY),) * 3,
        scratch_shapes=[
            vmem((tokens, features), BF16),
            vmem((features, tokens), BF16),
            vmem((c, features, w), BF16),
            vmem((c, own_tokens, w), BF16),
            vmem((c, 2, 4, own_tokens, w), BF16),
            vmem((c, 2, 2, own_tokens, h), BF16),
            vmem((c, 2, 2, own_tokens, w), BF16),
            vmem((c, own_tokens, w), BF16),
            vmem((c, own_tokens, w), BF16),
            vmem((c, own_tokens, w), F32),
            vmem((c, 2, 4, own_tokens, w), BF16),
            vmem((c, 8, own_features, w), BF16),
            vmem((c, 2, own_features, h), BF16),
            vmem((c, 3, 2, own_features, w), BF16),
            vmem((7, own_tokens, w), BF16),
            vmem((tokens, features), F32),
            vmem((4, col_tokens, features), BF16),
            vmem((3, col_tokens, features), BF16),
            vmem((col_tokens, features), BF16),
            vmem((c, own_tokens, w), BF16),
            vmem((c, own_features, w), BF16),
            dma((c, COPIES)),
            dma((c, COPIES)),
            dma((14,)),
            dma((14,)),
            dma((3,)),
            dma((3,)),
            dma((c,)),
            dma((c,)),
            dma,
            dma((c,)),
            dma((c,)),
            dma,
        ],
        compiler_params=pltpu.CompilerParams(
            collective_id=0, has_side_effects=True, vmem_limit_bytes=60 * 1024 * 1024
        ),
        cost_estimate=pl.CostEstimate(
            flops=6 * tokens * features * hidden,
            bytes_accessed=2 * (features * hidden + 2 * own_tokens * hidden + tokens * features),
            transcendentals=own_tokens * hidden,
        ),
    )(tokens_in, weight, cotangent)
    return pl.pallas_call(
        publish,
        out_shape=tuple(jax.ShapeDtypeStruct(result.shape, result.dtype) for result in results),
        in_specs=[pl.BlockSpec(memory_space=pl.ANY)] * 3,
        out_specs=(pl.BlockSpec(memory_space=pl.ANY),) * 3,
        scratch_shapes=[vmem(result.shape, result.dtype) for result in results] + [dma((3,)), dma((3,))],
    )(*results)


def solution(mesh):
    in_specs = (P("dep", None, "row"), P("row", "col"), P("dep", "row", "col"))
    out_specs = (P("dep", "row", "col"), P("dep", "col", "row"), P(("row", "dep"), "col"))
    return jax.shard_map(
        body, mesh=mesh, in_specs=in_specs, out_specs=out_specs, check_vma=False
    )
```

```python
import functools
import math

import jax
import jax.numpy as jnp
from jax import lax
from jax.experimental import pallas as pl
from jax.experimental.pallas import tpu as pltpu
from jax.sharding import PartitionSpec as P

MESH = pl.DeviceIdType.MESH
F32 = jnp.float32
BF16 = jnp.bfloat16

WIDTH = 512

root_coef = math.sqrt(2.0 / math.pi)

RS1, RS2, RSY, AG1, AG2, AG3, Z1, Z2, Z3, Z4 = 0, 2, 4, 5, 8, 12, 13, 15, 17, 19
COPIES = 21

PLAN = (
    1, 2, 33, 384, 34, 65, 3, 97, 66, 35, 192, 129, 98, 4, 161, 67, 256, 130, 36, 193, 99, 5, 162, 288,
    68, 224, 257, 131, 37, 194, 100, 320, 6, 163, 289, 69, 225, 258, 132, 38, 195, 352, 101, 321, 7,
    164, 290, 70, 226, 259, 133, 39, 196, 353, 102, 322, 8, 165, 291, 71, 227, 260, 134, 40, 197, 354,
    103, 323, 9, 166, 292, 72, 228, 261, 135, 41, 198, 355, 104, 324, 10, 167, 293, 73, 229, 262, 136,
    42, 199, 356, 105, 325, 11, 168, 294, 74, 230, 263, 137, 43, 200, 357, 106, 326, 169, 295, 75, 231,
    264, 138, 201, 358, 107, 327, 170, 296, 232, 265, 139, 202, 359, 328, 171, 297, 233, 266, 203, 235,
    360, 329, 298, 234, 267, 361, 330, 299, 362, 331, 363,
)
STAGE_OF_INPUT_PART = 7
LAST_INPUT_PART = [entry % 32 for entry in PLAN if entry // 32 == STAGE_OF_INPUT_PART][-1]


def kernel(
    scale, chunks,
    tok_hbm, w_hbm, cot_hbm, act_hbm, ig_hbm, wg_hbm,
    tok, tok_t, w, cot, part, r1, r2, y_out, y_in, own, hid, grad, z1_in, z_in, direct_in,
    acc, ig_out, ig_in, ig_own, act, wg,
    send, recv, direct_send, direct_recv, col_send, col_recv, load_w, load_cot, load_tok,
    store_act, store_wg, store_ig,
):
    width = w.shape[2]
    half = width // 2
    left_half, right_half = pl.ds(0, half), pl.ds(half, half)
    row, col, dep = lax.axis_index("row"), lax.axis_index("col"), lax.axis_index("dep")
    x, y = lax.rem(row, 4), row // 4
    other_y = 1 - y
    xr, xo, xl = lax.rem(x + 1, 4), lax.rem(x + 2, 4), lax.rem(x + 3, 4)
    right, left = {"row": y * 4 + xr}, {"row": y * 4 + xl}
    across = {"row": other_y * 4 + x}
    at = [lax.rem(dep + k, 8) for k in range(8)]
    up, down = {"dep": at[1]}, {"dep": at[7]}
    row_peers = [(lax.rem(y + k // 4, 2), lax.rem(x + k % 4, 4)) for k in (6, 2, 5, 7, 1, 3, 4)]
    row_from = [(lax.rem(y + k // 4, 2), lax.rem(x + 4 - k % 4, 4)) for k in (6, 2, 5, 7, 1, 3, 4)]
    col_peers = [{"col": lax.rem(col + j, 4)} for j in (1, 2, 3)]

    def columns(c):
        return pl.ds(pl.multiple_of(c * width, 128), width)

    def tok_copy():
        return pltpu.make_async_copy(tok_hbm.at[0], tok, load_tok)

    def w_copy(c):
        return pltpu.make_async_copy(w_hbm.at[:, columns(c)], w.at[c], load_w.at[c])

    def cot_copy(c):
        return pltpu.make_async_copy(cot_hbm.at[0, :, columns(c)], cot.at[c], load_cot.at[c])

    tok_copy().start()

    @pl.loop(0, chunks)
    def _(c):
        w_copy(c).start()
        cot_copy(c).start()

    barrier = pltpu.get_barrier_semaphore()
    peers = [up, down] + [{"row": there_y * 4 + there_x} for there_y, there_x in row_peers] + col_peers
    for peer in peers:
        pl.semaphore_signal(barrier, inc=1, device_id=peer, device_id_type=MESH)

    def act_copy(c):
        return pltpu.make_async_copy(act.at[c], act_hbm.at[0, :, columns(c)], store_act.at[c])

    def wg_copy(c):
        return pltpu.make_async_copy(wg.at[c], wg_hbm.at[:, columns(c)], store_wg.at[c])

    def ig_copy():
        return pltpu.make_async_copy(ig_own, ig_hbm.at[0], store_ig)

    def remote(c, which, source, target, device):
        return pltpu.make_async_remote_copy(
            src_ref=source, dst_ref=target, send_sem=send.at[c, which], recv_sem=recv.at[c, which],
            device_id=device, device_id_type=MESH,
        )

    def direct(k, source, target):
        there_y, there_x = row_peers[k % 7]
        return pltpu.make_async_remote_copy(
            src_ref=source, dst_ref=target, send_sem=direct_send.at[k], recv_sem=direct_recv.at[k],
            device_id={"row": there_y * 4 + there_x}, device_id_type=MESH,
        )

    def direct_scatter():
        return [direct(k, part.at[0, *row_peers[k]], direct_in.at[k]) for k in range(7)]

    def direct_gather():
        return [direct(7 + k, hid.at[0, y, x], hid.at[0, y, x]) for k in range(7)]

    def direct_gathered():
        return [direct(7 + k, hid.at[0, *row_from[k]], hid.at[0, *row_from[k]]) for k in range(7)]

    def rs1(c):
        return (
            remote(c, RS1, part.at[c, :, xo, :, left_half], r1.at[c, 0], right),
            remote(c, RS1 + 1, part.at[c, :, xo, :, right_half], r1.at[c, 1], left),
        )

    def rs2(c):
        return (
            remote(c, RS2, part.at[c, :, xr], r2.at[c, 0], right),
            remote(c, RS2 + 1, part.at[c, :, xl], r2.at[c, 1], left),
        )

    def rsy(c):
        return (remote(c, RSY, y_out.at[c], y_in.at[c], across),)

    def block(c, which, there, device, columns=None):
        ref = hid.at[c, *there] if columns is None else hid.at[c, *there, :, columns]
        return remote(c, which, ref, ref, device)

    def ag1(c, here=True):
        return (
            block(c, AG1, (y, x if here else xl), right),
            block(c, AG1 + 1, (y, x if here else xr), left),
            block(c, AG1 + 2, (y if here else other_y, x), across),
        )

    def ag2(c, here=True):
        return (
            block(c, AG2, (y, xl if here else xo), right, left_half),
            block(c, AG2 + 1, (y, xr if here else xo), left, right_half),
            block(c, AG2 + 2, (y if here else other_y, xl), across),
            block(c, AG2 + 3, (y if here else other_y, xr), across),
        )

    def ag3(c, here=True):
        return (block(c, AG3, (y if here else other_y, xo), across),)

    def z1(c):
        return (
            remote(c, Z1, grad.at[c, at[4], :, left_half], z1_in.at[c, 0], up),
            remote(c, Z1 + 1, grad.at[c, at[4], :, right_half], z1_in.at[c, 1], down),
        )

    def z_step(c, which, step, above, below):
        return (
            remote(c, which, grad.at[c, above], z_in.at[c, step, 0], up),
            remote(c, which + 1, grad.at[c, below], z_in.at[c, step, 1], down),
        )

    def z2(c):
        return z_step(c, Z2, 0, at[3], at[5])

    def z3(c):
        return z_step(c, Z3, 1, at[2], at[6])

    def z4(c):
        return z_step(c, Z4, 2, at[1], at[7])

    def start(copies):
        for copy in copies:
            copy.start()

    def arrived(copies):
        for copy in copies:
            copy.wait_recv()

    def col_copy(j):
        return pltpu.make_async_remote_copy(
            src_ref=ig_out.at[lax.rem(col + j, 4)], dst_ref=ig_in.at[j - 1],
            send_sem=col_send.at[j - 1], recv_sem=col_recv.at[j - 1],
            device_id=col_peers[j - 1], device_id_type=MESH,
        )

    def f32(value):
        return value.astype(F32)

    def product_of(c):
        w_copy(c).wait()
        value = jnp.dot(tok[...], w[c], preferred_element_type=F32).astype(BF16)
        part[c] = value.reshape(part.shape[1:])

    def finish(c, value):
        square = value * value
        tangent = jnp.tanh(root_coef * (value + 0.044715 * value * square))
        slope = 0.5 * (1.0 + tangent) + 0.5 * value * (1.0 - tangent * tangent) * root_coef * (
            1.0 + 3.0 * 0.044715 * square
        )
        cot_copy(c).wait()
        hid[c, y, x] = (f32(cot[c]) * slope).astype(BF16)
        start(direct_gather() if isinstance(c, int) else ag1(c))
        act[c] = (0.5 * value * (1.0 + tangent)).astype(BF16)
        act_copy(c).start()

    def project(c):
        product_of(c)
        start(rs1(c))

    def row_second(c):
        arrived(rs1(c))
        part[c, :, xr, :, left_half] = (f32(part[c, :, xr, :, left_half]) + f32(r1[c, 0])).astype(BF16)
        part[c, :, xl, :, right_half] = (f32(part[c, :, xl, :, right_half]) + f32(r1[c, 1])).astype(BF16)
        start(rs2(c))

    def row_across(c):
        arrived(rs2(c))
        y_out[c] = (f32(part[c, other_y, x]) + f32(r2[c, 0, other_y]) + f32(r2[c, 1, other_y])).astype(BF16)
        start(rsy(c))
        own[c] = f32(part[c, y, x]) + f32(r2[c, 0, y]) + f32(r2[c, 1, y])

    def activate(c):
        arrived(rsy(c))
        finish(c, own[c] + f32(y_in[c]))

    def gather_second(c):
        arrived(ag1(c, False)[:2])
        start(ag2(c))

    def gather_third(c):
        arrived(ag2(c, False)[:2])
        start(ag3(c))

    def weight_first(c):
        @pl.when(c > 0)
        def _():
            arrived(ag1(c, False)[2:] + ag2(c, False)[2:] + ag3(c, False))

        @pl.when(c == 0)
        def _():
            arrived(direct_gathered())

        rows = hid[c].reshape(-1, width)
        product = jnp.dot(tok_t[...], rows, preferred_element_type=F32)
        grad[c] = (product * scale).astype(BF16).reshape(grad.shape[1:])
        start(z1(c))

    def input_part(c):
        rows = hid[c].reshape(-1, width)
        acc[...] += lax.dot_general(rows, w[c], (((1,), (1,)), ((), ())), preferred_element_type=F32)

        @pl.when(c == LAST_INPUT_PART)
        def _():
            ig_out[...] = acc[...].astype(BF16).reshape(ig_out.shape)
            for j in (1, 2, 3):
                col_copy(j).start()

    def weight_second(c):
        arrived(z1(c))
        grad[c, at[3], :, left_half] = (f32(grad[c, at[3], :, left_half]) + f32(z1_in[c, 0])).astype(BF16)
        grad[c, at[5], :, right_half] = (f32(grad[c, at[5], :, right_half]) + f32(z1_in[c, 1])).astype(BF16)
        start(z2(c))

    def weight_third(c):
        arrived(z2(c))
        grad[c, at[2]] = (f32(grad[c, at[2]]) + f32(z_in[c, 0, 0])).astype(BF16)
        grad[c, at[6]] = (f32(grad[c, at[6]]) + f32(z_in[c, 0, 1])).astype(BF16)
        start(z3(c))

    def weight_fourth(c):
        arrived(z3(c))
        grad[c, at[1]] = (f32(grad[c, at[1]]) + f32(z_in[c, 1, 0])).astype(BF16)
        grad[c, at[7]] = (f32(grad[c, at[7]]) + f32(z_in[c, 1, 1])).astype(BF16)
        start(z4(c))

    def weight_last(c):
        arrived(z4(c))
        wg[c] = (f32(grad[c, dep]) + f32(z_in[c, 2, 0]) + f32(z_in[c, 2, 1])).astype(BF16)
        wg_copy(c).start()

        def sent(stages_of_chunk):
            for copies in stages_of_chunk:
                for copy in copies(c):
                    copy.wait_send()

        sent((z1, z2, z3, z4))

        @pl.when(c > 0)
        def _():
            sent((rs1, rs2, rsy, ag1, ag2, ag3))

        @pl.when(c == 0)
        def _():
            for copy in direct_scatter() + direct_gather():
                copy.wait_send()

        act_copy(c).wait()

    def first_activate(_):
        arrived(direct_scatter())
        value = f32(part[0, y, x])
        for k in range(7):
            value = value + f32(direct_in[k])
        finish(0, value)

    tok_copy().wait()
    product_of(0)
    pl.semaphore_wait(barrier, len(peers))
    start(direct_scatter())
    tok_t[...] = tok[...].T
    acc[...] = jnp.zeros_like(acc)

    stages = (
        project, row_second, row_across, activate, gather_second, gather_third, weight_first,
        input_part, weight_second, weight_third, weight_fourth, weight_last, first_activate,
    )

    idle = 32 * len(stages)
    padded = list(PLAN) + [idle] * (-len(PLAN) % 12)
    words = [sum(entry * 512 ** k for k, entry in enumerate(padded[i:i + 3])) for i in range(0, len(padded), 3)]
    stages = stages + (lambda c: None,)

    def pick(place, values):
        while len(values) > 1:
            odd = lax.rem(place, 2) == 1
            pairs = [values[k:k + 2] for k in range(0, len(values), 2)]
            values = [jnp.where(odd, pair[-1], pair[0]) for pair in pairs]
            place = place // 2
        return values[0]

    def perform(i, group_words):
        word, within = pick(i // 3, group_words), lax.rem(i, 3)
        word = jnp.where(within == 0, word, jnp.where(within == 1, word // 512, word // 262144))
        entry = lax.rem(word, 512)
        stage, c = entry // 32, lax.rem(entry, 32)

        def dispatch(low, high):
            if high - low == 1:
                stages[low](c)
                return
            middle = (low + high) // 2
            lax.cond(stage < middle, lambda: dispatch(low, middle), lambda: dispatch(middle, high))

        dispatch(0, len(stages))

    @pl.loop(0, len(padded) // 12)
    def _(group):
        group_words = [pick(group, words[k::4]) for k in range(4)]
        pl.loop(0, 12)(lambda i: perform(i, group_words))

    for j in (1, 2, 3):
        col_copy(j).wait_recv()
    tokens = ig_own.shape[0]
    mine = acc[pl.ds(pl.multiple_of(col * tokens, 8), tokens), :]
    ig_own[...] = (mine + f32(ig_in[0]) + f32(ig_in[1]) + f32(ig_in[2])).astype(BF16)
    ig_copy().start()

    @pl.loop(0, chunks)
    def _(c):
        wg_copy(c).wait()

    for j in (1, 2, 3):
        col_copy(j).wait_send()
    ig_copy().wait()


def publish(act_from, ig_from, wg_from, act_to, ig_to, wg_to, act, ig, wg, sem_in, sem_out):
    inward, outward = [], []
    for k, (source, held, target) in enumerate(((wg_from, wg, wg_to), (act_from, act, act_to), (ig_from, ig, ig_to))):
        inward.append(pltpu.make_async_copy(source, held, sem_in.at[k]))
        outward.append(pltpu.make_async_copy(held, target, sem_out.at[k]))
    for copy in inward:
        copy.start()
    for copy, onward in zip(inward, outward):
        copy.wait()
        onward.start()
    for copy in outward:
        copy.wait()


def body(tokens_in, weight, cotangent):
    tokens, features = tokens_in.shape[1:]
    hidden = weight.shape[1]
    own_tokens = cotangent.shape[1]
    scale = 1.0 / math.sqrt(tokens * lax.axis_size("dep"))
    c, w = hidden // WIDTH, WIDTH
    h = w // 2
    own_features, col_tokens = features // 8, tokens // 4
    vmem = pltpu.VMEM
    dma = pltpu.SemaphoreType.DMA
    results = pl.pallas_call(
        functools.partial(kernel, scale, c),
        out_shape=(
            jax.ShapeDtypeStruct((1, own_tokens, hidden), BF16),
            jax.ShapeDtypeStruct((1, col_tokens, features), BF16),
            jax.ShapeDtypeStruct((own_features, hidden), BF16),
        ),
        in_specs=[pl.BlockSpec(memory_space=pl.ANY)] * 3,
        out_specs=(pl.BlockSpec(memory_space=pl.ANY),) * 3,
        scratch_shapes=[
            vmem((tokens, features), BF16),
            vmem((features, tokens), BF16),
            vmem((c, features, w), BF16),
            vmem((c, own_tokens, w), BF16),
            vmem((c, 2, 4, own_tokens, w), BF16),
            vmem((c, 2, 2, own_tokens, h), BF16),
            vmem((c, 2, 2, own_tokens, w), BF16),
            vmem((c, own_tokens, w), BF16),
            vmem((c, own_tokens, w), BF16),
            vmem((c, own_tokens, w), F32),
            vmem((c, 2, 4, own_tokens, w), BF16),
            vmem((c, 8, own_features, w), BF16),
            vmem((c, 2, own_features, h), BF16),
            vmem((c, 3, 2, own_features, w), BF16),
            vmem((7, own_tokens, w), BF16),
            vmem((tokens, features), F32),
            vmem((4, col_tokens, features), BF16),
            vmem((3, col_tokens, features), BF16),
            vmem((col_tokens, features), BF16),
            vmem((c, own_tokens, w), BF16),
            vmem((c, own_features, w), BF16),
            dma((c, COPIES)),
            dma((c, COPIES)),
            dma((14,)),
            dma((14,)),
            dma((3,)),
            dma((3,)),
            dma((c,)),
            dma((c,)),
            dma,
            dma((c,)),
            dma((c,)),
            dma,
        ],
        compiler_params=pltpu.CompilerParams(
            collective_id=0, has_side_effects=True, vmem_limit_bytes=60 * 1024 * 1024
        ),
        cost_estimate=pl.CostEstimate(
            flops=6 * tokens * features * hidden,
            bytes_accessed=2 * (features * hidden + 2 * own_tokens * hidden + tokens * features),
            transcendentals=own_tokens * hidden,
        ),
    )(tokens_in, weight, cotangent)
    return pl.pallas_call(
        publish,
        out_shape=tuple(jax.ShapeDtypeStruct(result.shape, result.dtype) for result in results),
        in_specs=[pl.BlockSpec(memory_space=pl.ANY)] * 3,
        out_specs=(pl.BlockSpec(memory_space=pl.ANY),) * 3,
        scratch_shapes=[vmem(result.shape, result.dtype) for result in results] + [dma((3,)), dma((3,))],
    )(*results)


def solution(mesh):
    in_specs = (P("dep", None, "row"), P("row", "col"), P("dep", "row", "col"))
    out_specs = (P("dep", "row", "col"), P("dep", "col", "row"), P(("row", "dep"), "col"))
    return jax.shard_map(
        body, mesh=mesh, in_specs=in_specs, out_specs=out_specs, check_vma=False
    )
```

```python
import functools
import math

import jax
import jax.numpy as jnp
from jax import lax
from jax.experimental import pallas as pl
from jax.experimental.pallas import tpu as pltpu
from jax.sharding import PartitionSpec as P

MESH = pl.DeviceIdType.MESH
F32 = jnp.float32
BF16 = jnp.bfloat16

WIDTH = 512

root_coef = math.sqrt(2.0 / math.pi)

RS1, RS2, RSY, AG1, AG2, AG3, Z1, Z2, Z3, Z4 = 0, 2, 4, 5, 8, 12, 13, 15, 17, 19
COPIES = 21

PLAN = (
    1, 2, 33, 384, 34, 65, 3, 97, 66, 35, 192, 129, 98, 4, 161, 67, 256, 130, 36, 193, 99, 5, 162, 288,
    68, 224, 257, 131, 37, 194, 100, 320, 6, 163, 289, 69, 225, 258, 132, 38, 195, 352, 101, 321, 7,
    164, 290, 70, 226, 259, 133, 39, 196, 353, 102, 322, 8, 165, 291, 71, 227, 260, 134, 40, 197, 354,
    103, 323, 9, 166, 292, 72, 228, 261, 135, 41, 198, 355, 104, 324, 10, 167, 293, 73, 229, 262, 136,
    42, 199, 356, 105, 325, 11, 168, 294, 74, 230, 263, 137, 43, 200, 357, 106, 326, 169, 295, 75, 231,
    264, 138, 201, 358, 107, 327, 170, 296, 232, 265, 139, 202, 359, 328, 171, 297, 233, 266, 203, 235,
    360, 329, 298, 234, 267, 361, 330, 299, 362, 331, 363,
)
STAGE_OF_INPUT_PART = 7
LAST_INPUT_PART = [entry % 32 for entry in PLAN if entry // 32 == STAGE_OF_INPUT_PART][-1]


def kernel(
    scale, chunks,
    tok_hbm, w_hbm, cot_hbm, act_hbm, ig_hbm, wg_hbm,
    tok, tok_t, w, cot, part, r1, r2, y_out, y_in, own, hid, grad, z1_in, z_in, direct_in,
    acc, ig_out, ig_in, ig_own, act, wg,
    send, recv, direct_send, direct_recv, col_send, col_recv, load_w, load_cot, load_tok,
    store_act, store_wg, store_ig,
):
    width = w.shape[2]
    half = width // 2
    left_half, right_half = pl.ds(0, half), pl.ds(half, half)
    row, col, dep = lax.axis_index("row"), lax.axis_index("col"), lax.axis_index("dep")
    x, y = lax.rem(row, 4), row // 4
    other_y = 1 - y
    xr, xo, xl = lax.rem(x + 1, 4), lax.rem(x + 2, 4), lax.rem(x + 3, 4)
    right, left = {"row": y * 4 + xr}, {"row": y * 4 + xl}
    across = {"row": other_y * 4 + x}
    at = [lax.rem(dep + k, 8) for k in range(8)]
    up, down = {"dep": at[1]}, {"dep": at[7]}
    row_peers = [(lax.rem(y + k // 4, 2), lax.rem(x + k % 4, 4)) for k in (6, 2, 5, 7, 1, 3, 4)]
    row_from = [(lax.rem(y + k // 4, 2), lax.rem(x + 4 - k % 4, 4)) for k in (6, 2, 5, 7, 1, 3, 4)]
    col_peers = [{"col": lax.rem(col + j, 4)} for j in (1, 2, 3)]

    def columns(c):
        return pl.ds(pl.multiple_of(c * width, 128), width)

    def tok_copy():
        return pltpu.make_async_copy(tok_hbm.at[0], tok, load_tok)

    def w_copy(c):
        return pltpu.make_async_copy(w_hbm.at[:, columns(c)], w.at[c], load_w.at[c])

    def cot_copy(c):
        return pltpu.make_async_copy(cot_hbm.at[0, :, columns(c)], cot.at[c], load_cot.at[c])

    tok_copy().start()

    @pl.loop(0, chunks)
    def _(c):
        w_copy(c).start()
        cot_copy(c).start()

    barrier = pltpu.get_barrier_semaphore()
    peers = [up, down] + [{"row": there_y * 4 + there_x} for there_y, there_x in row_peers] + col_peers
    for peer in peers:
        pl.semaphore_signal(barrier, inc=1, device_id=peer, device_id_type=MESH)

    def act_copy(c):
        return pltpu.make_async_copy(act.at[c], act_hbm.at[0, :, columns(c)], store_act.at[c])

    def wg_copy(c):
        return pltpu.make_async_copy(wg.at[c], wg_hbm.at[:, columns(c)], store_wg.at[c])

    def ig_copy():
        return pltpu.make_async_copy(ig_own, ig_hbm.at[0], store_ig)

    def remote(c, which, source, target, device):
        return pltpu.make_async_remote_copy(
            src_ref=source, dst_ref=target, send_sem=send.at[which],
            recv_sem=recv.at[c if isinstance(c, jax.Array) else 0, which],
            device_id=device, device_id_type=MESH,
        )

    def direct(k, source, target):
        there_y, there_x = row_peers[k % 7]
        return pltpu.make_async_remote_copy(
            src_ref=source, dst_ref=target, send_sem=direct_send.at[k], recv_sem=direct_recv.at[k],
            device_id={"row": there_y * 4 + there_x}, device_id_type=MESH,
        )

    def direct_scatter():
        return [direct(k, part.at[0, *row_peers[k]], direct_in.at[k]) for k in range(7)]

    def direct_gather():
        return [direct(7 + k, hid.at[0, y, x], hid.at[0, y, x]) for k in range(7)]

    def direct_gathered():
        return [direct(7 + k, hid.at[0, *row_from[k]], hid.at[0, *row_from[k]]) for k in range(7)]

    def rs1(c):
        return (
            remote(c, RS1, part.at[c, :, xo, :, left_half], r1.at[c, 0], right),
            remote(c, RS1 + 1, part.at[c, :, xo, :, right_half], r1.at[c, 1], left),
        )

    def rs2(c):
        return (
            remote(c, RS2, part.at[c, :, xr], r2.at[c, 0], right),
            remote(c, RS2 + 1, part.at[c, :, xl], r2.at[c, 1], left),
        )

    def rsy(c):
        return (remote(c, RSY, y_out.at[c], y_in.at[c], across),)

    def block(c, which, there, device, columns=None):
        ref = hid.at[c, *there] if columns is None else hid.at[c, *there, :, columns]
        return remote(c, which, ref, ref, device)

    def ag1(c, here=True):
        return (
            block(c, AG1, (y, x if here else xl), right),
            block(c, AG1 + 1, (y, x if here else xr), left),
            block(c, AG1 + 2, (y if here else other_y, x), across),
        )

    def ag2(c, here=True):
        return (
            block(c, AG2, (y, xl if here else xo), right, left_half),
            block(c, AG2 + 1, (y, xr if here else xo), left, right_half),
            block(c, AG2 + 2, (y if here else other_y, xl), across),
            block(c, AG2 + 3, (y if here else other_y, xr), across),
        )

    def ag3(c, here=True):
        return (block(c, AG3, (y if here else other_y, xo), across),)

    def z1(c):
        return (
            remote(c, Z1, grad.at[c, at[4], :, left_half], z1_in.at[c, 0], up),
            remote(c, Z1 + 1, grad.at[c, at[4], :, right_half], z1_in.at[c, 1], down),
        )

    def z_step(c, which, step, above, below):
        return (
            remote(c, which, grad.at[c, above], z_in.at[c, step, 0], up),
            remote(c, which + 1, grad.at[c, below], z_in.at[c, step, 1], down),
        )

    def z2(c):
        return z_step(c, Z2, 0, at[3], at[5])

    def z3(c):
        return z_step(c, Z3, 1, at[2], at[6])

    def z4(c):
        return z_step(c, Z4, 2, at[1], at[7])

    def start(copies):
        for copy in copies:
            copy.start()

    def arrived(copies):
        for copy in copies:
            copy.wait_recv()

    def col_copy(j):
        return pltpu.make_async_remote_copy(
            src_ref=ig_out.at[lax.rem(col + j, 4)], dst_ref=ig_in.at[j - 1],
            send_sem=col_send.at[j - 1], recv_sem=col_recv.at[j - 1],
            device_id=col_peers[j - 1], device_id_type=MESH,
        )

    def f32(value):
        return value.astype(F32)

    def product_of(c):
        w_copy(c).wait()
        value = jnp.dot(tok[...], w[c], preferred_element_type=F32).astype(BF16)
        part[c] = value.reshape(part.shape[1:])

    def finish(c, value):
        square = value * value
        tangent = jnp.tanh(root_coef * (value + 0.044715 * value * square))
        slope = 0.5 * (1.0 + tangent) + 0.5 * value * (1.0 - tangent * tangent) * root_coef * (
            1.0 + 3.0 * 0.044715 * square
        )
        cot_copy(c).wait()
        hid[c, y, x] = (f32(cot[c]) * slope).astype(BF16)
        start(direct_gather() if isinstance(c, int) else ag1(c))
        act[c] = (0.5 * value * (1.0 + tangent)).astype(BF16)
        act_copy(c).start()

    def project(c):
        product_of(c)
        start(rs1(c))

    def row_second(c):
        arrived(rs1(c))
        part[c, :, xr, :, left_half] = (f32(part[c, :, xr, :, left_half]) + f32(r1[c, 0])).astype(BF16)
        part[c, :, xl, :, right_half] = (f32(part[c, :, xl, :, right_half]) + f32(r1[c, 1])).astype(BF16)
        start(rs2(c))

    def row_across(c):
        arrived(rs2(c))
        y_out[c] = (f32(part[c, other_y, x]) + f32(r2[c, 0, other_y]) + f32(r2[c, 1, other_y])).astype(BF16)
        start(rsy(c))
        own[c] = f32(part[c, y, x]) + f32(r2[c, 0, y]) + f32(r2[c, 1, y])

    def activate(c):
        arrived(rsy(c))
        finish(c, own[c] + f32(y_in[c]))

    def gather_second(c):
        arrived(ag1(c, False)[:2])
        start(ag2(c))

    def gather_third(c):
        arrived(ag2(c, False)[:2])
        start(ag3(c))

    def weight_first(c):
        @pl.when(c > 0)
        def _():
            arrived(ag1(c, False)[2:] + ag2(c, False)[2:] + ag3(c, False))

        @pl.when(c == 0)
        def _():
            arrived(direct_gathered())

        rows = hid[c].reshape(-1, width)
        product = jnp.dot(tok_t[...], rows, preferred_element_type=F32)
        grad[c] = (product * scale).astype(BF16).reshape(grad.shape[1:])
        start(z1(c))

    def input_part(c):
        rows = hid[c].reshape(-1, width)
        acc[...] += lax.dot_general(rows, w[c], (((1,), (1,)), ((), ())), preferred_element_type=F32)

        @pl.when(c == LAST_INPUT_PART)
        def _():
            ig_out[...] = acc[...].astype(BF16).reshape(ig_out.shape)
            for j in (1, 2, 3):
                col_copy(j).start()

    def weight_second(c):
        arrived(z1(c))
        grad[c, at[3], :, left_half] = (f32(grad[c, at[3], :, left_half]) + f32(z1_in[c, 0])).astype(BF16)
        grad[c, at[5], :, right_half] = (f32(grad[c, at[5], :, right_half]) + f32(z1_in[c, 1])).astype(BF16)
        start(z2(c))

    def weight_third(c):
        arrived(z2(c))
        grad[c, at[2]] = (f32(grad[c, at[2]]) + f32(z_in[c, 0, 0])).astype(BF16)
        grad[c, at[6]] = (f32(grad[c, at[6]]) + f32(z_in[c, 0, 1])).astype(BF16)
        start(z3(c))

    def weight_fourth(c):
        arrived(z3(c))
        grad[c, at[1]] = (f32(grad[c, at[1]]) + f32(z_in[c, 1, 0])).astype(BF16)
        grad[c, at[7]] = (f32(grad[c, at[7]]) + f32(z_in[c, 1, 1])).astype(BF16)
        start(z4(c))

    def weight_last(c):
        arrived(z4(c))
        wg[c] = (f32(grad[c, dep]) + f32(z_in[c, 2, 0]) + f32(z_in[c, 2, 1])).astype(BF16)
        wg_copy(c).start()

    def first_activate(_):
        arrived(direct_scatter())
        value = f32(part[0, y, x])
        for k in range(7):
            value = value + f32(direct_in[k])
        finish(0, value)

    tok_copy().wait()
    product_of(0)
    pl.semaphore_wait(barrier, len(peers))
    start(direct_scatter())
    tok_t[...] = tok[...].T
    acc[...] = jnp.zeros_like(acc)

    stages = (
        project, row_second, row_across, activate, gather_second, gather_third, weight_first,
        input_part, weight_second, weight_third, weight_fourth, weight_last, first_activate,
    )

    words = [
        sum(entry * 512 ** k for k, entry in enumerate(PLAN[i:i + 3])) for i in range(0, len(PLAN), 3)
    ]

    @pl.loop(0, len(PLAN))
    def _(i):
        place, level = i // 3, words
        while len(level) > 1:
            odd = lax.rem(place, 2) == 1
            pairs = [level[k:k + 2] for k in range(0, len(level), 2)]
            level = [jnp.where(odd, pair[-1], pair[0]) for pair in pairs]
            place = place // 2
        within = lax.rem(i, 3)
        word = jnp.where(within == 0, level[0], jnp.where(within == 1, level[0] // 512, level[0] // 262144))
        entry = lax.rem(word, 512)
        stage, c = entry // 32, lax.rem(entry, 32)

        def dispatch(low, high):
            if high - low == 1:
                stages[low](c)
                return
            middle = (low + high) // 2
            lax.cond(stage < middle, lambda: dispatch(low, middle), lambda: dispatch(middle, high))

        dispatch(0, len(stages))

    for j in (1, 2, 3):
        col_copy(j).wait_recv()
    tokens = ig_own.shape[0]
    mine = acc[pl.ds(pl.multiple_of(col * tokens, 8), tokens), :]
    ig_own[...] = (mine + f32(ig_in[0]) + f32(ig_in[1]) + f32(ig_in[2])).astype(BF16)
    ig_copy().start()

    rest, every = pl.ds(1, chunks - 1), pl.ds(0, chunks)
    for copies in (rs1, rs2, rsy, ag1, ag2, ag3):
        for copy in copies(rest):
            copy.wait_send()
    for copies in (z1, z2, z3, z4):
        for copy in copies(every):
            copy.wait_send()
    for copy in direct_scatter() + direct_gather():
        copy.wait_send()

    @pl.loop(0, chunks)
    def _(c):
        act_copy(c).wait()
        wg_copy(c).wait()

    for j in (1, 2, 3):
        col_copy(j).wait_send()
    ig_copy().wait()


def publish(act_from, ig_from, wg_from, act_to, ig_to, wg_to, act, ig, wg, sem_in, sem_out):
    inward, outward = [], []
    for k, (source, held, target) in enumerate(((wg_from, wg, wg_to), (act_from, act, act_to), (ig_from, ig, ig_to))):
        inward.append(pltpu.make_async_copy(source, held, sem_in.at[k]))
        outward.append(pltpu.make_async_copy(held, target, sem_out.at[k]))
    for copy in inward:
        copy.start()
    for copy, onward in zip(inward, outward):
        copy.wait()
        onward.start()
    for copy in outward:
        copy.wait()


def body(tokens_in, weight, cotangent):
    tokens, features = tokens_in.shape[1:]
    hidden = weight.shape[1]
    own_tokens = cotangent.shape[1]
    scale = 1.0 / math.sqrt(tokens * lax.axis_size("dep"))
    c, w = hidden // WIDTH, WIDTH
    h = w // 2
    own_features, col_tokens = features // 8, tokens // 4
    vmem = pltpu.VMEM
    dma = pltpu.SemaphoreType.DMA
    results = pl.pallas_call(
        functools.partial(kernel, scale, c),
        out_shape=(
            jax.ShapeDtypeStruct((1, own_tokens, hidden), BF16),
            jax.ShapeDtypeStruct((1, col_tokens, features), BF16),
            jax.ShapeDtypeStruct((own_features, hidden), BF16),
        ),
        in_specs=[pl.BlockSpec(memory_space=pl.ANY)] * 3,
        out_specs=(pl.BlockSpec(memory_space=pl.ANY),) * 3,
        scratch_shapes=[
            vmem((tokens, features), BF16),
            vmem((features, tokens), BF16),
            vmem((c, features, w), BF16),
            vmem((c, own_tokens, w), BF16),
            vmem((c, 2, 4, own_tokens, w), BF16),
            vmem((c, 2, 2, own_tokens, h), BF16),
            vmem((c, 2, 2, own_tokens, w), BF16),
            vmem((c, own_tokens, w), BF16),
            vmem((c, own_tokens, w), BF16),
            vmem((c, own_tokens, w), F32),
            vmem((c, 2, 4, own_tokens, w), BF16),
            vmem((c, 8, own_features, w), BF16),
            vmem((c, 2, own_features, h), BF16),
            vmem((c, 3, 2, own_features, w), BF16),
            vmem((7, own_tokens, w), BF16),
            vmem((tokens, features), F32),
            vmem((4, col_tokens, features), BF16),
            vmem((3, col_tokens, features), BF16),
            vmem((col_tokens, features), BF16),
            vmem((c, own_tokens, w), BF16),
            vmem((c, own_features, w), BF16),
            dma((COPIES,)),
            dma((c, COPIES)),
            dma((14,)),
            dma((14,)),
            dma((3,)),
            dma((3,)),
            dma((c,)),
            dma((c,)),
            dma,
            dma((c,)),
            dma((c,)),
            dma,
        ],
        compiler_params=pltpu.CompilerParams(
            collective_id=0, has_side_effects=True, vmem_limit_bytes=60 * 1024 * 1024
        ),
        cost_estimate=pl.CostEstimate(
            flops=6 * tokens * features * hidden,
            bytes_accessed=2 * (features * hidden + 2 * own_tokens * hidden + tokens * features),
            transcendentals=own_tokens * hidden,
        ),
    )(tokens_in, weight, cotangent)
    return pl.pallas_call(
        publish,
        out_shape=tuple(jax.ShapeDtypeStruct(result.shape, result.dtype) for result in results),
        in_specs=[pl.BlockSpec(memory_space=pl.ANY)] * 3,
        out_specs=(pl.BlockSpec(memory_space=pl.ANY),) * 3,
        scratch_shapes=[vmem(result.shape, result.dtype) for result in results] + [dma((3,)), dma((3,))],
    )(*results)


def solution(mesh):
    in_specs = (P("dep", None, "row"), P("row", "col"), P("dep", "row", "col"))
    out_specs = (P("dep", "row", "col"), P("dep", "col", "row"), P(("row", "dep"), "col"))
    return jax.shard_map(
        body, mesh=mesh, in_specs=in_specs, out_specs=out_specs, check_vma=False
    )
```
